256 devices in a mesh: grp: 2 (over x_lo), dp: 32 (over y, z), mp: 4 (over x_hi, core).
Axes of the slice: x: 4 (x_hi: 2, x_lo: 2; x = x_hi * 2 + x_lo), y: 4, z: 8, core: 2. Of those that a mesh axis runs over, the one named last changes fastest.
Arguments:
- pooled: bfloat16 [32, 8, 4096, 128], P('dp', ('grp', 'mp')), may hold values from -32 to 32
- counts: int32 [32, 8, 4096], P('dp', ('grp', 'mp')), may hold values from 0 to 7
- sample_order: int32 [8, 4096], P(('grp', 'mp')), may hold values from 0 to 4095, each once within a row
- table_order: int32 [32], replicated, may hold values from 0 to 31, each once
- teacher_w1: bfloat16 [4096, 2048], P(None, ('grp', 'mp')), may hold values from -0.09375 to 0.09375
- teacher_w2: bfloat16 [2048, 2048], P(('grp', 'mp')), may hold values from -0.125 to 0.125
- projection: bfloat16 [2048, 512], replicated, may hold values from -0.125 to 0.125
- student_w1: bfloat16 [4096, 512], replicated, may hold values from -0.09375 to 0.09375
- student_w2: bfloat16 [512, 512], replicated, may hold values from -0.25 to 0.25
Outputs:
- grad_w1: float32 [4096, 512], P(('grp', 'dp', 'mp'))
- grad_w2: float32 [512, 512], replicated
- sample_loss: float32 [8, 4096], P(('grp', 'mp'), 'dp')
The draws below stay inside these ranges and needn't reach their ends.
Inputs may be any that keep to these rules, and one draw needn't show every extreme that they name: `sample_order`: each row is a permutation; slot i of block q lies on dp index i // 128. `table_order`: a permutation; storage slot s lies on dp index s.
All inputs are finite; a program needn't handle non-finite values.
Results may differ from the reference program's by a relative error of at most 0.0085.
The reference program's roundings to bfloat16 on the way (of `averaged`, `ordered`, `features`, `teacher_hidden`, `student_hidden`, `out_grad` and `hidden_grad`) count: a program that leaves them out, or rounds other values in their place, can miss the bound.
Values may be sent and summed in bfloat16 or wider, within the bound.
No kernel may reach another device: no remote copies, remote signals or barrier semaphores. Data moves between devices by JAX's collectives and lax.ppermute only.
A program may use at most 128 MiB of HBM per device.

```python
import jax
import jax.numpy as jnp
from jax import lax

E = 128
TH = 2048
TOUT = 2048
SH = 512
SO = 512
TABLES = 32
BLOCK = 4096
GROUPS = 8


def touch_ends(array, rng, smallest, high):
    shape = array.shape
    place = [jax.random.randint(jax.random.fold_in(rng, axis), (), 0, shape[axis]) for axis in range(len(shape))]
    array = array.at[tuple(place)].set(smallest)
    longest = shape.index(max(shape))
    place[longest] = (place[longest] + 1) % shape[longest]
    return array.at[tuple(place)].set(high)


def raised(drawn, rng, source, target, shards_of, factor):
    def block_of(position):
        return (jnp.arange(drawn.shape[position]) // (drawn.shape[position] // shards_of)).reshape((-1,) + (1,) * (drawn.ndim - 1 - position))

    one_side = jax.random.permutation(rng, shards_of)[block_of(target)]
    second = (block_of(target) + shards_of // 2) % shards_of
    return jnp.where((block_of(source) == one_side) | (block_of(source) == second), factor * drawn, drawn)


def block_levels(key, shape, shards, low, high):
    gain, own = 1.0, jax.random.fold_in(key, 6)
    for position, parts in shards:
        draws = jnp.exp(jax.random.uniform(jax.random.fold_in(own, position), (parts,), jnp.float32, low / len(shards), high / len(shards)))
        gain = gain * jnp.repeat(draws, shape[position] // parts).reshape([-1 if axis == position else 1 for axis in range(len(shape))])
    return gain


def scatter_about(key, shape, spread, limit, pieces=(), held_as=jnp.bfloat16):
    values = jax.random.normal(key, shape, jnp.float32) * spread
    if len(pieces) > 0:
        values = block_levels(key, shape, pieces, -0.22, 0.18) * values
    return jnp.clip(values, min=-limit, max=limit).astype(held_as)


def bell_draw_with(own_key, dims, width, most, cuts, heavy, kind=jnp.bfloat16):
    result = width * jax.random.normal(own_key, dims, jnp.float32)
    if cuts:
        result = result * block_levels(own_key, dims, cuts, -0.22, 0.18)
    return jnp.clip(raised(result, jax.random.fold_in(own_key, 3), *heavy), -most, most).astype(kind)


def setup_inputs(seed: int = 0) -> dict:
    key_list = jax.random.split(jax.random.key(seed), 10)
    return {
        "pooled": bell_draw_with(key_list[0], (TABLES, GROUPS, BLOCK, E), 3.0, 32.0, ((0, 32), (1, 8)), (2, 0, 32, 2.75)),
        "counts": touch_ends(jax.random.randint(key_list[1], (TABLES, GROUPS, BLOCK), 0, 8), jax.random.fold_in(key_list[1], 1), 0, 7).astype(jnp.int32),
        "sample_order": jax.vmap(lambda own: jax.random.permutation(own, BLOCK))(jax.random.split(key_list[2], GROUPS)).reshape((GROUPS, BLOCK)).astype(jnp.int32),
        "table_order": jax.random.permutation(key_list[3], TABLES).astype(jnp.int32),
        "teacher_w1": scatter_about(key_list[4], (TABLES * E, TH), (TABLES * E) ** -0.5, 0.09375, ((1, 8),)),
        "teacher_w2": scatter_about(key_list[5], (TH, TOUT), TH ** -0.5, 0.125, ((0, 8),)),
        "projection": scatter_about(key_list[6], (TOUT, SO), TOUT ** -0.5, 0.125),
        "student_w1": scatter_about(key_list[7], (TABLES * E, SH), (TABLES * E) ** -0.5, 0.09375),
        "student_w2": scatter_about(key_list[8], (SH, SO), SH ** -0.5, 0.25),
    }


def reference(pooled, counts, sample_order, table_order, teacher_w1, teacher_w2, projection, student_w1, student_w2):
    divisor = jnp.maximum(counts, 1).astype(jnp.float32)
    averaged = (pooled.astype(jnp.float32) / divisor[..., None]).astype(jnp.bfloat16)
    ordered = jnp.take_along_axis(averaged, sample_order[None, :, :, None].astype(jnp.int32), axis=2)
    inverse = jnp.zeros((TABLES,), jnp.int32).at[table_order].set(jnp.arange(TABLES, dtype=jnp.int32))
    canonical = jnp.take(ordered, inverse, axis=0)
    features = jnp.transpose(canonical, (1, 2, 0, 3)).reshape(GROUPS * BLOCK, TABLES * E)
    teacher_hidden = jax.nn.relu(jnp.dot(features, teacher_w1, preferred_element_type=jnp.float32)).astype(jnp.bfloat16)
    teacher_rows = jnp.dot(teacher_hidden, teacher_w2, preferred_element_type=jnp.float32)
    target = jnp.dot(teacher_rows, projection.astype(jnp.float32), precision=lax.Precision.HIGHEST)
    student_pre = jnp.dot(features, student_w1, preferred_element_type=jnp.float32)
    student_hidden = jax.nn.relu(student_pre).astype(jnp.bfloat16)
    student_out = jnp.dot(student_hidden, student_w2, preferred_element_type=jnp.float32)
    difference = student_out - target
    sample_loss = (0.5 * jnp.mean(difference * difference, axis=1)).reshape(GROUPS, BLOCK)
    grad_scale = 8192.0 / (GROUPS * BLOCK * SO)
    out_grad = (grad_scale * difference).astype(jnp.bfloat16)
    grad_w2 = jnp.dot(student_hidden.T, out_grad, preferred_element_type=jnp.float32)
    back = jnp.dot(out_grad, student_w2.T, preferred_element_type=jnp.float32)
    hidden_grad = jnp.where(student_pre > 0, back, 0.0).astype(jnp.bfloat16)
    grad_w1 = jnp.dot(features.T, hidden_grad, preferred_element_type=jnp.float32)
    return grad_w1, grad_w2, sample_loss
```

```python
import jax
import jax.numpy as jnp
from jax import lax
from jax.experimental import pallas as pl
from jax.experimental.pallas import tpu as pltpu
from jax.sharding import PartitionSpec as P

LINE = ("grp", "mp")
CHUNKS = 2


def dot(left, right):
    return jnp.dot(left, right, preferred_element_type=jnp.float32)


def contract_rows(left, right):
    return lax.dot_general(
        left, right, (((0,), (0,)), ((), ())), preferred_element_type=jnp.float32
    )


def place(x, core):
    x = x % 4
    return (x % 2) * 4 + (x // 2) * 2 + core


def shift(values, steps, swap=0):
    pairs = [
        (place(x, core), place(x + steps, core ^ swap)) for x in range(4) for core in range(2)
    ]
    return lax.ppermute(values, LINE, pairs)


def gather_line(values):
    half = values.shape[0] // 2
    found = {(0, 0): values, (1, 0): shift(values, 1), (-1, 0): shift(values, -1)}
    found[(0, 1)] = shift(values, 0, 1)
    upper = shift(found[(1, 0)][:half], 1)
    lower = shift(found[(-1, 0)][half:], -1)
    found[(1, 1)] = shift(found[(1, 0)], 0, 1)
    found[(-1, 1)] = shift(found[(-1, 0)], 0, 1)
    found[(2, 0)] = jnp.concatenate([upper, lower], axis=0)
    found[(2, 1)] = shift(found[(2, 0)], 0, 1)
    return found


def gather_line_small(values):
    found = {(0, 0): values}
    for steps in (1, -1, 2):
        found[(steps, 0)] = shift(values, steps)
    for steps in (0, 1, -1, 2):
        found[(steps, 1)] = shift(found[(steps, 0)], 0, 1)
    return found


SPOTS = ((0, 0), (0, 1), (1, 0), (1, 1), (-1, 0), (-1, 1), (2, 0), (2, 1))
WAVES = (SPOTS[:2], SPOTS[2:6], SPOTS[6:])


def arrange_kernel(inverse_ref, arrived_ref, features_ref):
    tables, _, width = arrived_ref.shape
    for column in range(tables):
        features_ref[:, column * width : (column + 1) * width] = arrived_ref[inverse_ref[column]]


def arrange(arrived, inverse):
    tables, rows, width = arrived.shape
    return pl.pallas_call(
        arrange_kernel,
        out_shape=jax.ShapeDtypeStruct((rows, tables * width), arrived.dtype),
        in_specs=[
            pl.BlockSpec(memory_space=pltpu.SMEM),
            pl.BlockSpec(memory_space=pltpu.VMEM),
        ],
        out_specs=pl.BlockSpec(memory_space=pltpu.VMEM),
        compiler_params=pltpu.CompilerParams(vmem_limit_bytes=16 * 1024 * 1024),
    )(inverse, arrived)


def split_two(values):
    upper = lax.optimization_barrier(values.astype(jnp.bfloat16))
    lower = (values - upper.astype(jnp.float32)).astype(jnp.bfloat16)
    return jnp.concatenate([upper, lower], axis=0)


def shards(
    pooled,
    counts,
    sample_order,
    table_order,
    teacher_w1,
    teacher_w2,
    projection,
    student_w1,
    student_w2,
):
    group = lax.axis_index("grp")
    member = lax.axis_index("mp")
    tables = table_order.shape[0]
    block, width = pooled.shape[2:]
    samples = block // tables
    part = samples // CHUNKS
    hidden = teacher_w1.shape[1]
    inner = student_w2.shape[0]
    outer = student_w2.shape[1]

    inverse = jnp.sum(
        jnp.where(
            table_order[None, :] == jnp.arange(tables, dtype=jnp.int32)[:, None],
            jnp.arange(tables, dtype=jnp.int32)[None, :],
            0,
        ),
        axis=1,
    )

    joined = split_two(dot(teacher_w2, projection))
    joined = gather_line_small(joined)

    divisor = jnp.maximum(counts[0, 0], 1).astype(jnp.float32)
    averaged = (pooled[0, 0].astype(jnp.float32) / divisor[:, None]).astype(jnp.bfloat16)
    order = sample_order[0].reshape(tables, CHUNKS, part)
    features, lines = [], []
    for chunk in range(CHUNKS):
        outgoing = averaged.at[order[:, chunk].reshape(-1)].get(mode="promise_in_bounds")
        arrived = lax.all_to_all(
            outgoing.reshape(tables, part, width), "dp", split_axis=0, concat_axis=0, tiled=True
        )
        features.append(arrange(arrived, inverse))
        lines.append(gather_line(features[-1]))

    returned = {}
    stacked = []
    for chunk in range(CHUNKS):
        for wave in WAVES:
            rows = jnp.concatenate([lines[chunk][spot] for spot in wave], axis=0)
            stacked.append(rows)
            held = jax.nn.relu(dot(rows, teacher_w1)).astype(jnp.bfloat16)
            for index, (steps, swap) in enumerate(wave):
                mine = held[index * part : (index + 1) * part]
                if (steps, swap) != (0, 0):
                    mine = shift(mine, -steps, swap)
                returned[(chunk, steps, swap)] = mine

    hiddens = jnp.concatenate(
        [
            jnp.concatenate([returned[(chunk, steps, swap)] for chunk in range(CHUNKS)], axis=0)
            for steps, swap in SPOTS
        ],
        axis=1,
    )
    away = {(steps, swap): (-steps if abs(steps) == 1 else steps, swap) for steps, swap in SPOTS}
    upper = jnp.concatenate([joined[away[spot]][:hidden] for spot in SPOTS], axis=0)
    lower = jnp.concatenate([joined[away[spot]][hidden:] for spot in SPOTS], axis=0)
    target = dot(hiddens, upper) + dot(hiddens, lower)

    own = jnp.concatenate(features, axis=0)
    student_pre = dot(own, student_w1)
    student_hidden = jax.nn.relu(student_pre).astype(jnp.bfloat16)
    difference = dot(student_hidden, student_w2) - target
    sample_loss = (0.5 * jnp.mean(difference * difference, axis=1)).reshape(1, samples)
    devices = lax.axis_size("grp") * lax.axis_size("dp") * lax.axis_size("mp")
    grad_scale = 8192.0 / (samples * devices * outer)
    out_grad = (grad_scale * difference).astype(jnp.bfloat16)
    back = lax.dot_general(
        out_grad, student_w2, (((1,), (1,)), ((), ())), preferred_element_type=jnp.float32
    )
    hidden_grad = jnp.where(student_pre > 0, back, 0.0).astype(jnp.bfloat16)

    hidden_line = gather_line_small(student_hidden)
    out_line = gather_line_small(out_grad)
    second = contract_rows(
        jnp.concatenate([hidden_line[spot] for spot in SPOTS], axis=0),
        jnp.concatenate([out_line[spot] for spot in SPOTS], axis=0),
    )
    rank = group * lax.axis_size("mp") + member
    slab = inner // 8
    second = lax.dynamic_slice_in_dim(second, rank * slab, slab, axis=0)
    second = lax.all_to_all(
        second.reshape(tables, slab // tables, outer), "dp", split_axis=0, concat_axis=0, tiled=True
    )
    second = jnp.sum(second, axis=0)
    second = lax.all_to_all(
        jnp.broadcast_to(second[None], (tables,) + second.shape),
        "dp",
        split_axis=0,
        concat_axis=0,
        tiled=True,
    ).reshape(slab, outer)
    seconds = gather_line_small(second)
    chip = 2 * (member // 2) + group
    core = member % 2
    grad_w2 = jnp.zeros((inner, outer), jnp.float32)
    for steps, swap in SPOTS:
        x = (chip - steps) % 4
        spot = (x % 2) * 4 + (x // 2) * 2 + (core ^ swap)
        grad_w2 = lax.dynamic_update_slice_in_dim(
            grad_w2, seconds[(steps, swap)], spot * slab, axis=0
        )

    grad_line = gather_line_small(hidden_grad)
    grads = []
    for chunk in range(CHUNKS):
        for wave in WAVES:
            grads.extend(grad_line[spot][chunk * part : (chunk + 1) * part] for spot in wave)
    stacked = jnp.concatenate(stacked, axis=0)
    span = tables * width // 2
    stacked = lax.dynamic_slice_in_dim(stacked, group * span, span, axis=1)
    first = contract_rows(stacked, jnp.concatenate(grads, axis=0))
    rows = span // (tables * 4)
    first = first.reshape(tables, 4, rows, inner)
    first = lax.dynamic_index_in_dim(first, member, axis=1, keepdims=False).astype(jnp.bfloat16)
    first = lax.all_to_all(first, "dp", split_axis=0, concat_axis=0, tiled=True)
    grad_w1 = jnp.sum(first.astype(jnp.float32), axis=0)
    return (grad_w1, grad_w2, sample_loss)


def solution(mesh):
    return jax.shard_map(
        shards,
        mesh=mesh,
        in_specs=(
            P("dp", LINE, None, None),
            P("dp", LINE, None),
            P(LINE, None),
            P(),
            P(None, LINE),
            P(LINE, None),
            P(),
            P(),
            P(),
        ),
        out_specs=(P(("grp", "dp", "mp"), None), P(), P(LINE, "dp")),
        check_vma=False,
    )
```

```python
import jax
import jax.numpy as jnp
from jax import lax
from jax.experimental import pallas as pl
from jax.experimental.pallas import tpu as pltpu
from jax.sharding import PartitionSpec as P

LINE = ("grp", "mp")
CORE, NEAR, FAR, OPPOSITE = 1, 4, 6, 2

smem = pl.BlockSpec(memory_space=pltpu.SMEM)
vmem = pl.BlockSpec(memory_space=pltpu.VMEM)
LIMIT = pltpu.CompilerParams(vmem_limit_bytes=40 * 1024 * 1024)


def dot(left, right):
    return jnp.dot(left, right, preferred_element_type=jnp.float32)


def swap(values, mask):
    return lax.ppermute(values, LINE, [(index, index ^ mask) for index in range(8)])


def split_two(values):
    upper = lax.optimization_barrier(values.astype(jnp.bfloat16))
    lower = (values - upper.astype(jnp.float32)).astype(jnp.bfloat16)
    return jnp.concatenate([upper, lower], axis=0)


def order_kernel(order_ref, averaged_ref, ordered_ref):
    step = 64

    @pl.loop(0, ordered_ref.shape[0] // step)
    def _(index):
        base = pl.multiple_of(index * step, step)
        rows = [averaged_ref[pl.ds(order_ref[0, base + row], 1), :] for row in range(step)]
        ordered_ref[pl.ds(base, step), :] = jnp.concatenate(rows, axis=0).astype(jnp.bfloat16)


def take_rows(averaged, order):
    return pl.pallas_call(
        order_kernel,
        out_shape=jax.ShapeDtypeStruct(averaged.shape, jnp.bfloat16),
        in_specs=[smem, vmem],
        out_specs=vmem,
        compiler_params=LIMIT,
        name="take_rows",
    )(order, averaged)


def arrange_kernel(inverse_ref, arrived_ref, features_ref):
    tables, _, width = arrived_ref.shape
    for column in range(tables):
        features_ref[:, column * width : (column + 1) * width] = arrived_ref[inverse_ref[column]]


def arrange(arrived, inverse):
    tables, rows, width = arrived.shape
    return pl.pallas_call(
        arrange_kernel,
        out_shape=jax.ShapeDtypeStruct((rows, tables * width), arrived.dtype),
        in_specs=[smem, vmem],
        out_specs=vmem,
        compiler_params=LIMIT,
        name="arrange",
    )(inverse, arrived)


def teacher_kernel(features_ref, first, second, third, fourth, joined_ref, joined_core_ref, out_ref):
    hidden = first.shape[1]
    total = None
    for weights, joined, base in (
        (first, joined_ref, 0),
        (second, joined_ref, 2 * hidden),
        (third, joined_core_ref, 0),
        (fourth, joined_core_ref, 2 * hidden),
    ):
        held = jnp.maximum(dot(features_ref[...], weights[...]), 0.0).astype(jnp.bfloat16)
        term = dot(held, joined[base : base + hidden, :])
        term = term + dot(held, joined[base + hidden : base + 2 * hidden, :])
        total = term if total is None else total + term
    out_ref[...] = total


def teacher(features, weights, joined, joined_core):
    return pl.pallas_call(
        teacher_kernel,
        out_shape=jax.ShapeDtypeStruct((features.shape[0], joined.shape[1]), jnp.float32),
        in_specs=[vmem] * 7,
        out_specs=vmem,
        compiler_params=LIMIT,
        name="teacher",
    )(features, *weights, joined, joined_core)


def student_kernel(scale, out_ref, here_ref, there_ref, pre_ref, weights_ref, loss_ref, grads_ref):
    width = out_ref.shape[1]
    difference = out_ref[...] - (here_ref[...] + there_ref[...])
    loss_ref[...] = 0.5 * jnp.mean(difference * difference, axis=1, keepdims=True)
    out_grad = (scale * difference).astype(jnp.bfloat16)
    grads_ref[:, :width] = out_grad
    back = lax.dot_general(
        out_grad, weights_ref[...], (((1,), (1,)), ((), ())), preferred_element_type=jnp.float32
    )
    grads_ref[:, width:] = jnp.where(pre_ref[...] > 0, back, 0.0).astype(jnp.bfloat16)


def student(scale, student_out, here, there, student_pre, student_w2):
    samples, width = student_out.shape
    inner = student_pre.shape[1]
    return pl.pallas_call(
        lambda *refs: student_kernel(scale, *refs),
        out_shape=(
            jax.ShapeDtypeStruct((samples, 1), jnp.float32),
            jax.ShapeDtypeStruct((samples, width + inner), jnp.bfloat16),
        ),
        in_specs=[vmem] * 5,
        out_specs=(vmem, vmem),
        compiler_params=LIMIT,
        name="student",
    )(student_out, here, there, student_pre, student_w2)


def turn_kernel(spot_ref, own_ref, near_ref, far_ref, upper_ref, lower_ref, turned_ref):
    samples = own_ref.shape[0]
    span = own_ref.shape[1] // 2
    start = spot_ref[0] * span
    high = spot_ref[1]
    for column in range(span // 128):
        columns = pl.ds(pl.multiple_of(start + column * 128, 128), 128)
        blocks = [own_ref[:, columns], near_ref[:, columns], far_ref[:, columns]]
        blocks.append(jnp.concatenate([upper_ref[:, columns], lower_ref[:, columns]], axis=0))
        for piece, block in enumerate(blocks):
            turned = block.astype(jnp.float32).T
            for index in range(2):
                base = index * 64
                rows = jnp.where(
                    high == 0, turned[base : base + 32], turned[base + 32 : base + 64]
                ).astype(jnp.bfloat16)
                place = (2 * column + index) * 16
                for core in range(2):
                    turned_ref[
                        core, place : place + 16, piece * samples : (piece + 1) * samples
                    ] = rows[core * 16 : (core + 1) * 16]


def turn(spot, own, near, far, upper, lower):
    samples, depth = own.shape
    return pl.pallas_call(
        turn_kernel,
        out_shape=jax.ShapeDtypeStruct((2, depth // 8, 4 * samples), jnp.bfloat16),
        in_specs=[smem] + [vmem] * 5,
        out_specs=vmem,
        compiler_params=LIMIT,
        name="turn",
    )(spot, own, near, far, upper, lower)


def gradient_kernel(spot_ref, turned_ref, *refs):
    grads, hiddens, (mine_ref, other_ref) = refs[:4], refs[4:8], refs[8:]
    width = hiddens[0].shape[1]
    core = spot_ref[2]
    out_grad = jnp.concatenate([ref[:, :width] for ref in grads], axis=0)
    hidden_grad = jnp.concatenate([ref[:, width:] for ref in grads], axis=0)
    slab = pl.ds(pl.multiple_of((2 * spot_ref[0] + spot_ref[1]) * 128, 128), 128)
    hidden = jnp.concatenate([ref[:, slab] for ref in hiddens], axis=0)
    second = lax.dot_general(
        hidden, out_grad, (((0,), (0,)), ((), ())), preferred_element_type=jnp.float32
    )
    half = second.shape[0] // 2
    mine_ref[:half, :] = jnp.where(core == 0, second[:half], second[half:])
    other_ref[:half, :] = jnp.where(core == 0, second[half:], second[:half]).astype(jnp.bfloat16)
    mine_ref[half:, :] = dot(turned_ref[core], hidden_grad)
    other_ref[half:, :] = dot(turned_ref[1 - core], hidden_grad).astype(jnp.bfloat16)


def gradients(spot, turned, grads, hiddens):
    rows = turned.shape[1] + 64
    width = hiddens[0].shape[1]
    return pl.pallas_call(
        gradient_kernel,
        out_shape=(
            jax.ShapeDtypeStruct((rows, width), jnp.float32),
            jax.ShapeDtypeStruct((rows, width), jnp.bfloat16),
        ),
        in_specs=[smem] + [vmem] * 9,
        out_specs=(vmem, vmem),
        compiler_params=LIMIT,
        name="gradients",
    )(spot, turned, *grads, *hiddens)


def assemble_kernel(spot_ref, own_ref, near_ref, far_ref, opposite_ref, core_ref, out_ref):
    rows = own_ref.shape[0]
    group, high, core = spot_ref[0], spot_ref[1], spot_ref[2]
    for index, (ref, at) in enumerate(
        (
            (own_ref, 2 * group + high),
            (near_ref, 2 * (1 - group) + high),
            (far_ref, 2 * (1 - group) + 1 - high),
            (opposite_ref, 2 * group + 1 - high),
        )
    ):
        here = pl.multiple_of((2 * at + core) * rows, rows)
        there = pl.multiple_of((2 * at + 1 - core) * rows, rows)
        out_ref[pl.ds(here, rows), :] = ref[...]
        out_ref[pl.ds(there, rows), :] = core_ref[index * rows : (index + 1) * rows, :]


def assemble(spot, own, near, far, opposite, core):
    return pl.pallas_call(
        assemble_kernel,
        out_shape=jax.ShapeDtypeStruct((8 * own.shape[0], own.shape[1]), jnp.float32),
        in_specs=[smem] + [vmem] * 5,
        out_specs=vmem,
        compiler_params=LIMIT,
        name="assemble",
    )(spot, own, near, far, opposite, core)


def shards(
    pooled,
    counts,
    sample_order,
    table_order,
    teacher_w1,
    teacher_w2,
    projection,
    student_w1,
    student_w2,
):
    group = lax.axis_index("grp")
    member = lax.axis_index("mp")
    spot = jnp.stack([group, member // 2, member % 2]).astype(jnp.int32)
    tables = table_order.shape[0]
    block, width = pooled.shape[2:]
    samples = block // tables
    inner, outer = student_w2.shape

    near_w1 = swap(teacher_w1, NEAR)
    joined = split_two(dot(teacher_w2, projection))
    joined = jnp.concatenate([joined, swap(joined, NEAR)], axis=0)
    joined_core = swap(joined, CORE)
    weights = (teacher_w1, near_w1, swap(teacher_w1, CORE), swap(near_w1, CORE))

    table_range = jnp.arange(tables, dtype=jnp.int32)
    inverse = jnp.sum(
        jnp.where(table_order[None, :] == table_range[:, None], table_range[None, :], 0), axis=1
    )
    divisor = jnp.maximum(counts[0, 0], 1).astype(jnp.float32)
    averaged = pooled[0, 0].astype(jnp.float32) / divisor[:, None]
    ordered = take_rows(averaged, sample_order)
    arrived = lax.all_to_all(
        ordered.reshape(tables, samples, width), "dp", split_axis=0, concat_axis=0, tiled=True
    )
    own = arrange(arrived, inverse)
    far = swap(own, FAR)
    near = swap(own, NEAR)

    there = swap(teacher(far, weights, joined, joined_core), FAR)
    here = teacher(own, weights, joined, joined_core)

    student_pre = dot(own, student_w1)
    student_hidden = jax.nn.relu(student_pre).astype(jnp.bfloat16)
    student_out = dot(student_hidden, student_w2)
    hiddens = [student_hidden] + [swap(student_hidden, mask) for mask in (NEAR, FAR, OPPOSITE)]

    devices = lax.axis_size("grp") * lax.axis_size("dp") * lax.axis_size("mp")
    grad_scale = 8192.0 / (samples * devices * outer)
    sample_loss, grads = student(grad_scale, student_out, here, there, student_pre, student_w2)
    grads = [grads] + [swap(grads, mask) for mask in (NEAR, FAR, OPPOSITE)]

    upper = swap(near[: samples // 2], FAR)
    lower = swap(far[samples // 2 :], NEAR)
    turned = turn(spot, own, near, far, upper, lower)

    mine, other = gradients(spot, turned, grads, hiddens)
    mine = mine + swap(other, CORE).astype(jnp.float32)
    slab = inner // 8
    second = lax.all_to_all(
        mine[:slab].reshape(tables, slab // tables, outer),
        "dp",
        split_axis=0,
        concat_axis=0,
        tiled=True,
    )
    first = lax.all_to_all(
        mine[slab:].astype(jnp.bfloat16).reshape(tables, -1, inner),
        "dp",
        split_axis=0,
        concat_axis=0,
        tiled=True,
    )
    grad_w1 = jnp.sum(first.astype(jnp.float32), axis=0)
    second = jnp.sum(second, axis=0)
    second = lax.all_to_all(
        jnp.broadcast_to(second[None], (tables,) + second.shape),
        "dp",
        split_axis=0,
        concat_axis=0,
        tiled=True,
    ).reshape(slab, outer)
    seconds = [second] + [swap(second, mask) for mask in (NEAR, FAR, OPPOSITE)]
    grad_w2 = assemble(spot, *seconds, swap(jnp.concatenate(seconds, axis=0), CORE))
    return (grad_w1, grad_w2, sample_loss.reshape(1, samples))


def solution(mesh):
    return jax.shard_map(
        shards,
        mesh=mesh,
        in_specs=(
            P("dp", LINE, None, None),
            P("dp", LINE, None),
            P(LINE, None),
            P(),
            P(None, LINE),
            P(LINE, None),
            P(),
            P(),
            P(),
        ),
        out_specs=(P(("grp", "dp", "mp"), None), P(), P(LINE, "dp")),
        check_vma=False,
    )
```

```python
import jax
import jax.numpy as jnp
from jax import lax
from jax.experimental import pallas as pl
from jax.experimental.pallas import tpu as pltpu
from jax.sharding import PartitionSpec as P

LINE = ("grp", "mp")
CORE, NEAR, FAR, OPPOSITE = 1, 4, 6, 2

smem = pl.BlockSpec(memory_space=pltpu.SMEM)
vmem = pl.BlockSpec(memory_space=pltpu.VMEM)
anywhere = pl.BlockSpec(memory_space=pl.ANY)


def limit(mebibytes):
    return pltpu.CompilerParams(vmem_limit_bytes=mebibytes * 1024 * 1024)


def tie(*values):
    return lax.optimization_barrier(values)


def dot(left, right):
    return jnp.dot(left, right, preferred_element_type=jnp.float32)


def swap(values, mask):
    return lax.ppermute(values, LINE, [(index, index ^ mask) for index in range(8)])


def split_two(values):
    upper = lax.optimization_barrier(values.astype(jnp.bfloat16))
    lower = (values - upper.astype(jnp.float32)).astype(jnp.bfloat16)
    return jnp.concatenate([upper, lower], axis=0)


def across(values):
    return lax.all_to_all(values, "dp", split_axis=0, concat_axis=0, tiled=True)


def total_of(values, parts):
    return jnp.sum(values.reshape(parts, -1, values.shape[1]).astype(jnp.float32), axis=0)


def order_kernel(order_ref, averaged_ref, ordered_ref):
    step = 64

    @pl.loop(0, ordered_ref.shape[0] // step)
    def _(index):
        base = pl.multiple_of(index * step, step)
        rows = [averaged_ref[pl.ds(order_ref[0, base + row], 1), :] for row in range(step)]
        ordered_ref[pl.ds(base, step), :] = jnp.concatenate(rows, axis=0).astype(jnp.bfloat16)


def take_rows(averaged, order):
    return pl.pallas_call(
        order_kernel,
        out_shape=jax.ShapeDtypeStruct(averaged.shape, jnp.bfloat16),
        in_specs=[smem, vmem],
        out_specs=vmem,
        compiler_params=limit(8),
        name="take_rows",
    )(order, averaged)


def arrange_kernel(inverse_ref, arrived_ref, features_ref, semaphores):
    tables, _, width = arrived_ref.shape
    copies = [
        pltpu.make_async_copy(
            arrived_ref.at[inverse_ref[column]],
            features_ref.at[:, column * width : (column + 1) * width],
            semaphores.at[column],
        )
        for column in range(tables)
    ]
    for copy in copies:
        copy.start()
    for copy in copies:
        copy.wait()


def arrange(arrived, inverse):
    tables, rows, width = arrived.shape
    return pl.pallas_call(
        arrange_kernel,
        out_shape=jax.ShapeDtypeStruct((rows, tables * width), arrived.dtype),
        in_specs=[smem, pl.BlockSpec(memory_space=pltpu.HBM)],
        out_specs=vmem,
        scratch_shapes=[pltpu.SemaphoreType.DMA((tables,))],
        compiler_params=limit(6),
        name="arrange",
    )(inverse, arrived)


def teacher_kernel(features_ref, *refs):
    joined, weights, before, out_ref = refs[:2], refs[2:4], refs[4:-1], refs[-1]
    total = before[0][...] if before else None
    for joined_ref, weights_ref in zip(joined, weights):
        hidden = weights_ref.shape[1]
        held = jnp.maximum(dot(features_ref[...], weights_ref[...]), 0.0).astype(jnp.bfloat16)
        term = dot(held, joined_ref[:hidden, :]) + dot(held, joined_ref[hidden:, :])
        total = term if total is None else total + term
    out_ref[...] = total


def teacher(features, weights, joined, *before):
    return pl.pallas_call(
        teacher_kernel,
        out_shape=jax.ShapeDtypeStruct((features.shape[0], joined[0].shape[1]), jnp.float32),
        in_specs=[vmem] * (5 + len(before)),
        out_specs=vmem,
        compiler_params=limit(10),
        cost_estimate=pl.CostEstimate(flops=0, bytes_accessed=0, transcendentals=0),
        name="teacher",
    )(features, *joined, *weights, *before)


def student_kernel(
    scale, out_ref, here_ref, there_ref, pre_ref, hidden_ref, weights_ref, loss_ref, grad_ref, second_ref
):
    width = out_ref.shape[1]
    difference = out_ref[...] - (here_ref[...] + there_ref[...])
    out_grad = (scale * difference).astype(jnp.bfloat16)
    back = lax.dot_general(
        out_grad, weights_ref[...], (((1,), (1,)), ((), ())), preferred_element_type=jnp.float32
    )
    grad_ref[...] = jnp.where(pre_ref[...] > 0, back, 0.0).astype(jnp.bfloat16)
    second_ref[...] = lax.dot_general(
        hidden_ref[...], out_grad, (((0,), (0,)), ((), ())), preferred_element_type=jnp.float32
    ).astype(jnp.bfloat16)
    square = difference * difference
    total = square[:, :128]
    for column in range(128, width, 128):
        total = total + square[:, column : column + 128]
    loss_ref[...] = (0.5 / width) * jnp.sum(total.T, axis=0, keepdims=True)


def student(scale, student_out, here, there, student_pre, student_hidden, student_w2):
    samples, width = student_out.shape
    inner = student_pre.shape[1]
    return pl.pallas_call(
        lambda *refs: student_kernel(scale, *refs),
        out_shape=(
            jax.ShapeDtypeStruct((1, samples), jnp.float32),
            jax.ShapeDtypeStruct((samples, inner), jnp.bfloat16),
            jax.ShapeDtypeStruct((inner, width), jnp.bfloat16),
        ),
        in_specs=[vmem] * 6,
        out_specs=(vmem,) * 3,
        compiler_params=limit(8),
        name="student",
    )(student_out, here, there, student_pre, student_hidden, student_w2)


def turn_kernel(spot_ref, *refs):
    pieces, turned_ref = refs[:-1], refs[-1]
    span = pieces[0].shape[1] // 2
    start = spot_ref[0] * span
    high = spot_ref[1]
    for column in range(span // 128):
        columns = pl.ds(pl.multiple_of(start + column * 128, 128), 128)
        rows = jnp.concatenate([ref[:, columns] for ref in pieces], axis=0)
        for block in range(rows.shape[0] // 128):
            samples = slice(block * 128, (block + 1) * 128)
            turned = rows[samples].astype(jnp.float32).T
            for index in range(2):
                base = index * 64
                kept = jnp.where(
                    high == 0, turned[base : base + 32], turned[base + 32 : base + 64]
                ).astype(jnp.bfloat16)
                place = (2 * column + index) * 16
                for core in range(2):
                    turned_ref[core, place : place + 16, samples] = kept[core * 16 : core * 16 + 16]


def turn(spot, *pieces):
    samples = sum(piece.shape[0] for piece in pieces)
    return pl.pallas_call(
        turn_kernel,
        out_shape=jax.ShapeDtypeStruct((2, pieces[0].shape[1] // 8, samples), jnp.bfloat16),
        in_specs=[smem] + [vmem] * len(pieces),
        out_specs=vmem,
        compiler_params=limit(8),
        name="turn",
    )(spot, *pieces)


def gradient_kernel(spot_ref, early_ref, late_ref, *refs):
    grads, (mine_ref, other_ref) = refs[:4], refs[4:]
    core = spot_ref[2]
    grad = jnp.concatenate([ref[...] for ref in grads], axis=0)
    early = early_ref.shape[2]
    for ref, place in ((other_ref, 1 - core), (mine_ref, core)):
        total = dot(early_ref[place], grad[:early]) + dot(late_ref[place], grad[early:])
        ref[...] = total.astype(ref.dtype)


def gradients(spot, early, late, grads):
    shape = (early.shape[1], grads[0].shape[1])
    return pl.pallas_call(
        gradient_kernel,
        out_shape=(
            jax.ShapeDtypeStruct(shape, jnp.float32),
            jax.ShapeDtypeStruct(shape, jnp.bfloat16),
        ),
        in_specs=[smem] + [vmem] * 6,
        out_specs=(vmem, vmem),
        compiler_params=limit(8),
        name="gradients",
    )(spot, early, late, *grads)


def shards(
    pooled,
    counts,
    sample_order,
    table_order,
    teacher_w1,
    teacher_w2,
    projection,
    student_w1,
    student_w2,
):
    group = lax.axis_index("grp")
    member = lax.axis_index("mp")
    spot = jnp.stack([group, member // 2, member % 2]).astype(jnp.int32)
    tables = table_order.shape[0]
    block, width = pooled.shape[2:]
    samples = block // tables
    inner, outer = student_w2.shape

    near_w1 = swap(teacher_w1, NEAR)
    core_w1 = swap(teacher_w1, CORE)

    table_range = jnp.arange(tables, dtype=jnp.int32)
    inverse = jnp.sum(
        jnp.where(table_order[None, :] == table_range[:, None], table_range[None, :], 0), axis=1
    )
    divisor = jnp.maximum(counts[0, 0], 1).astype(jnp.float32)
    averaged = pooled[0, 0].astype(jnp.float32) / divisor[:, None]
    ordered = take_rows(averaged, sample_order)
    arrived = lax.all_to_all(
        ordered.reshape(tables, samples, width), "dp", split_axis=0, concat_axis=0, tiled=True
    )

    late_w2, _ = tie(teacher_w2, ordered)
    joined = split_two(dot(late_w2, projection))
    near_joined = swap(joined, NEAR)
    core_joined = swap(joined, CORE)
    near_w1, joined = tie(near_w1, joined)
    near_core_w1 = swap(near_w1, CORE)

    own = arrange(arrived, inverse)
    far = swap(own, FAR)
    near = swap(own, NEAR)

    student_pre = dot(own, student_w1)
    student_hidden = jax.nn.relu(student_pre).astype(jnp.bfloat16)
    student_out = dot(student_hidden, student_w2)
    chip = ((teacher_w1, core_w1), (joined, core_joined))
    here = teacher(own, *chip)

    far, near_joined, here, student_out = tie(far, near_joined, here, student_out)
    next_chip = ((near_w1, near_core_w1), (near_joined, swap(near_joined, CORE)))
    partial = teacher(far, *chip)
    partial = teacher(far, *next_chip, partial)
    there = swap(partial, FAR)
    opposite = swap(far, NEAR)
    later_own, _ = tie(own, partial)
    here = teacher(later_own, *next_chip, here)
    there, here, near = tie(there, here, near)
    early = turn(spot, own, near, far)

    devices = lax.axis_size("grp") * lax.axis_size("dp") * lax.axis_size("mp")
    grad_scale = 8192.0 / (samples * devices * outer)
    sample_loss, grad, second = student(
        grad_scale, student_out, here, there, student_pre, student_hidden, student_w2
    )
    grads = [grad] + [swap(grad, mask) for mask in (NEAR, FAR, OPPOSITE)]
    late = turn(spot, opposite)

    second = across(second)
    mine, other = gradients(spot, early, late, grads)
    first = (mine + swap(other, CORE).astype(jnp.float32)).astype(jnp.bfloat16)
    first, second = tie(first, second)
    grad_w1 = total_of(across(first), tables)
    second = total_of(second, tables)
    for mask in (NEAR, OPPOSITE, CORE):
        second = second + swap(second, mask)
    second = jnp.broadcast_to(second.astype(jnp.bfloat16)[None], (tables,) + second.shape)
    grad_w2 = across(second.reshape(inner, outer)).astype(jnp.float32)
    return (grad_w1, grad_w2, sample_loss)


def solution(mesh):
    return jax.shard_map(
        shards,
        mesh=mesh,
        in_specs=(
            P("dp", LINE, None, None),
            P("dp", LINE, None),
            P(LINE, None),
            P(),
            P(None, LINE),
            P(LINE, None),
            P(),
            P(),
            P(),
        ),
        out_specs=(P(("grp", "dp", "mp"), None), P(), P(LINE, "dp")),
        check_vma=False,
    )
```

```python
import jax
import jax.numpy as jnp
from jax import lax
from jax.experimental import pallas as pl
from jax.experimental.pallas import tpu as pltpu
from jax.sharding import PartitionSpec as P

LINE = ("grp", "mp")
CORE, NEAR, FAR, OPPOSITE = 1, 4, 6, 2

smem = pl.BlockSpec(memory_space=pltpu.SMEM)
vmem = pl.BlockSpec(memory_space=pltpu.VMEM)
anywhere = pl.BlockSpec(memory_space=pl.ANY)


def limit(mebibytes):
    return pltpu.CompilerParams(vmem_limit_bytes=mebibytes * 1024 * 1024)


def tie(*values):
    return lax.optimization_barrier(values)


def dot(left, right):
    return jnp.dot(left, right, preferred_element_type=jnp.float32)


def swap(values, mask):
    return lax.ppermute(values, LINE, [(index, index ^ mask) for index in range(8)])


def split_two(values):
    upper = lax.optimization_barrier(values.astype(jnp.bfloat16))
    lower = (values - upper.astype(jnp.float32)).astype(jnp.bfloat16)
    return jnp.concatenate([upper, lower], axis=0)


def across(values):
    return lax.all_to_all(values, "dp", split_axis=0, concat_axis=0, tiled=True)


def total_of(values, parts):
    return jnp.sum(values.reshape(parts, -1, values.shape[1]).astype(jnp.float32), axis=0)


def order_kernel(order_ref, averaged_ref, ordered_ref):
    step = 64

    @pl.loop(0, ordered_ref.shape[0] // step)
    def _(index):
        base = pl.multiple_of(index * step, step)
        rows = [averaged_ref[pl.ds(order_ref[0, base + row], 1), :] for row in range(step)]
        ordered_ref[pl.ds(base, step), :] = jnp.concatenate(rows, axis=0).astype(jnp.bfloat16)


def take_rows(averaged, order):
    return pl.pallas_call(
        order_kernel,
        out_shape=jax.ShapeDtypeStruct(averaged.shape, jnp.bfloat16),
        in_specs=[smem, vmem],
        out_specs=vmem,
        compiler_params=limit(8),
        name="take_rows",
    )(order, averaged)


def arrange_kernel(inverse_ref, arrived_ref, features_ref):
    tables, _, width = arrived_ref.shape
    for column in range(tables):
        features_ref[:, column * width : (column + 1) * width] = arrived_ref[inverse_ref[column]]


def arrange(arrived, inverse):
    tables, rows, width = arrived.shape
    return pl.pallas_call(
        arrange_kernel,
        out_shape=jax.ShapeDtypeStruct((rows, tables * width), arrived.dtype),
        in_specs=[smem, vmem],
        out_specs=vmem,
        compiler_params=limit(6),
        name="arrange",
    )(inverse, arrived)


def teacher_kernel(features_ref, *refs):
    joined, weights, before, out_ref = refs[:2], refs[2:4], refs[4:-1], refs[-1]
    total = before[0][...] if before else None
    for joined_ref, weights_ref in zip(joined, weights):
        hidden = weights_ref.shape[1]
        held = jnp.maximum(dot(features_ref[...], weights_ref[...]), 0.0).astype(jnp.bfloat16)
        term = dot(held, joined_ref[:hidden, :]) + dot(held, joined_ref[hidden:, :])
        total = term if total is None else total + term
    out_ref[...] = total.astype(out_ref.dtype)


def teacher(features, weights, joined, *before, kept=jnp.float32):
    return pl.pallas_call(
        teacher_kernel,
        out_shape=jax.ShapeDtypeStruct((features.shape[0], joined[0].shape[1]), kept),
        in_specs=[vmem] * (5 + len(before)),
        out_specs=vmem,
        compiler_params=limit(10),
        cost_estimate=pl.CostEstimate(flops=0, bytes_accessed=0, transcendentals=0),
        name="teacher",
    )(features, *joined, *weights, *before)


def student_kernel(
    scale, out_ref, here_ref, there_ref, pre_ref, hidden_ref, weights_ref, loss_ref, grad_ref, second_ref
):
    width = out_ref.shape[1]
    difference = out_ref[...] - (here_ref[...] + there_ref[...].astype(jnp.float32))
    out_grad = (scale * difference).astype(jnp.bfloat16)
    back = lax.dot_general(
        out_grad, weights_ref[...], (((1,), (1,)), ((), ())), preferred_element_type=jnp.float32
    )
    grad_ref[...] = jnp.where(pre_ref[...] > 0, back, 0.0).astype(jnp.bfloat16)
    second_ref[...] = lax.dot_general(
        hidden_ref[...], out_grad, (((0,), (0,)), ((), ())), preferred_element_type=jnp.float32
    ).astype(jnp.bfloat16)
    square = difference * difference
    total = square[:, :128]
    for column in range(128, width, 128):
        total = total + square[:, column : column + 128]
    loss_ref[...] = (0.5 / width) * jnp.sum(total.T, axis=0, keepdims=True)


def student(scale, student_out, here, there, student_pre, student_hidden, student_w2):
    samples, width = student_out.shape
    inner = student_pre.shape[1]
    return pl.pallas_call(
        lambda *refs: student_kernel(scale, *refs),
        out_shape=(
            jax.ShapeDtypeStruct((1, samples), jnp.float32),
            jax.ShapeDtypeStruct((samples, inner), jnp.bfloat16),
            jax.ShapeDtypeStruct((inner, width), jnp.bfloat16),
        ),
        in_specs=[vmem] * 6,
        out_specs=(vmem,) * 3,
        compiler_params=limit(8),
        name="student",
    )(student_out, here, there, student_pre, student_hidden, student_w2)


def turn_kernel(spot_ref, *refs):
    pieces, turned_ref = refs[:-1], refs[-1]
    span = pieces[0].shape[1] // 2
    start = spot_ref[0] * span
    high = spot_ref[1]
    for column in range(span // 128):
        columns = pl.ds(pl.multiple_of(start + column * 128, 128), 128)
        rows = jnp.concatenate([ref[:, columns] for ref in pieces], axis=0)
        for block in range(rows.shape[0] // 128):
            samples = slice(block * 128, (block + 1) * 128)
            turned = rows[samples].astype(jnp.float32).T
            for index in range(2):
                base = index * 64
                kept = jnp.where(
                    high == 0, turned[base : base + 32], turned[base + 32 : base + 64]
                ).astype(jnp.bfloat16)
                place = (2 * column + index) * 16
                for core in range(2):
                    turned_ref[core, place : place + 16, samples] = kept[core * 16 : core * 16 + 16]


def turn(spot, *pieces):
    samples = sum(piece.shape[0] for piece in pieces)
    return pl.pallas_call(
        turn_kernel,
        out_shape=jax.ShapeDtypeStruct((2, pieces[0].shape[1] // 8, samples), jnp.bfloat16),
        in_specs=[smem] + [vmem] * len(pieces),
        out_specs=vmem,
        compiler_params=limit(8),
        name="turn",
    )(spot, *pieces)


def gradient_kernel(spot_ref, early_ref, late_ref, *refs):
    grads, (mine_ref, other_ref) = refs[:4], refs[4:]
    core = spot_ref[2]
    grad = jnp.concatenate([ref[...] for ref in grads], axis=0)
    early = early_ref.shape[2]
    for ref, place in ((other_ref, 1 - core), (mine_ref, core)):
        total = dot(early_ref[place], grad[:early]) + dot(late_ref[place], grad[early:])
        ref[...] = total.astype(ref.dtype)


def gradients(spot, early, late, grads):
    shape = (early.shape[1], grads[0].shape[1])
    return pl.pallas_call(
        gradient_kernel,
        out_shape=(
            jax.ShapeDtypeStruct(shape, jnp.float32),
            jax.ShapeDtypeStruct(shape, jnp.bfloat16),
        ),
        in_specs=[smem] + [vmem] * 6,
        out_specs=(vmem, vmem),
        compiler_params=limit(8),
        name="gradients",
    )(spot, early, late, *grads)


def shards(
    pooled,
    counts,
    sample_order,
    table_order,
    teacher_w1,
    teacher_w2,
    projection,
    student_w1,
    student_w2,
):
    group = lax.axis_index("grp")
    member = lax.axis_index("mp")
    spot = jnp.stack([group, member // 2, member % 2]).astype(jnp.int32)
    tables = table_order.shape[0]
    block, width = pooled.shape[2:]
    samples = block // tables
    inner, outer = student_w2.shape

    near_w1 = swap(teacher_w1, NEAR)
    core_w1 = swap(teacher_w1, CORE)

    table_range = jnp.arange(tables, dtype=jnp.int32)
    inverse = jnp.sum(
        jnp.where(table_order[None, :] == table_range[:, None], table_range[None, :], 0), axis=1
    )
    divisor = jnp.maximum(counts[0, 0], 1).astype(jnp.float32)
    averaged = pooled[0, 0].astype(jnp.float32) / divisor[:, None]
    ordered = take_rows(averaged, sample_order)
    arrived = lax.all_to_all(
        ordered.reshape(tables, samples, width), "dp", split_axis=0, concat_axis=0, tiled=True
    )

    late_w2, _ = tie(teacher_w2, ordered)
    joined = split_two(dot(late_w2, projection))
    near_joined = swap(joined, NEAR)
    core_joined = swap(joined, CORE)
    arrived, near_w1, joined = tie(arrived, near_w1, joined)

    own = arrange(arrived, inverse)
    near_core_w1 = swap(near_w1, CORE)
    far = swap(own, FAR)
    near = swap(own, NEAR)

    student_pre = dot(own, student_w1)
    student_hidden = jax.nn.relu(student_pre).astype(jnp.bfloat16)
    student_out = dot(student_hidden, student_w2)
    chip = ((teacher_w1, core_w1), (joined, core_joined))
    here = teacher(own, *chip)

    far, near_joined, here, student_out = tie(far, near_joined, here, student_out)
    next_chip = ((near_w1, near_core_w1), (near_joined, swap(near_joined, CORE)))
    partial = teacher(far, *chip)
    partial = teacher(far, *next_chip, partial, kept=jnp.bfloat16)
    there = swap(partial, FAR)
    opposite = swap(far, NEAR)
    later_own, _ = tie(own, partial)
    here = teacher(later_own, *next_chip, here)
    there, here, near = tie(there, here, near)
    early = turn(spot, own, near, far)

    devices = lax.axis_size("grp") * lax.axis_size("dp") * lax.axis_size("mp")
    grad_scale = 8192.0 / (samples * devices * outer)
    sample_loss, grad, second = student(
        grad_scale, student_out, here, there, student_pre, student_hidden, student_w2
    )
    grads = [grad] + [swap(grad, mask) for mask in (NEAR, FAR, OPPOSITE)]
    opposite, early = tie(opposite, early)
    late = turn(spot, opposite)

    second = across(second)
    mine, other = gradients(spot, early, late, grads)
    first = (mine + swap(other, CORE).astype(jnp.float32)).astype(jnp.bfloat16)
    first, second = tie(first, second)
    first = across(first)
    second = total_of(second, tables)
    for mask in (NEAR, OPPOSITE, CORE):
        second = second + swap(second, mask)
    second, first = tie(second, first)
    grad_w1 = total_of(first, tables)
    count = second.shape[0] // 2
    second = lax.dynamic_slice_in_dim(second, spot[2] * count, count, axis=0).astype(jnp.bfloat16)
    second = across(jnp.broadcast_to(second[None], (tables, count, outer)))
    third = swap(second, CORE)
    grad_w2 = jnp.where(
        spot[2] == 0,
        jnp.concatenate([second, third], axis=1),
        jnp.concatenate([third, second], axis=1),
    ).astype(jnp.float32).reshape(inner, outer)
    return (grad_w1, grad_w2, sample_loss)


def solution(mesh):
    return jax.shard_map(
        shards,
        mesh=mesh,
        in_specs=(
            P("dp", LINE, None, None),
            P("dp", LINE, None),
            P(LINE, None),
            P(),
            P(None, LINE),
            P(LINE, None),
            P(),
            P(),
            P(),
        ),
        out_specs=(P(("grp", "dp", "mp"), None), P(), P(LINE, "dp")),
        check_vma=False,
    )
```

```python
import jax
import jax.numpy as jnp
from jax import lax
from jax.experimental import pallas as pl
from jax.experimental.pallas import tpu as pltpu
from jax.sharding import PartitionSpec as P

LINE = ("grp", "mp")
CORE, NEAR, FAR, OPPOSITE = 1, 4, 6, 2

smem = pl.BlockSpec(memory_space=pltpu.SMEM)
vmem = pl.BlockSpec(memory_space=pltpu.VMEM)
anywhere = pl.BlockSpec(memory_space=pl.ANY)


def limit(mebibytes):
    return pltpu.CompilerParams(vmem_limit_bytes=mebibytes * 1024 * 1024)


def tie(*values):
    return lax.optimization_barrier(values)


def dot(left, right):
    return jnp.dot(left, right, preferred_element_type=jnp.float32)


def swap(values, mask):
    return lax.ppermute(values, LINE, [(index, index ^ mask) for index in range(8)])


def split_two(values):
    upper = lax.optimization_barrier(values.astype(jnp.bfloat16))
    lower = (values - upper.astype(jnp.float32)).astype(jnp.bfloat16)
    return jnp.concatenate([upper, lower], axis=0)


def across(values):
    return lax.all_to_all(values, "dp", split_axis=0, concat_axis=0, tiled=True)


def total_of(values, parts):
    return jnp.sum(values.reshape(parts, -1, values.shape[1]).astype(jnp.float32), axis=0)


def order_kernel(order_ref, averaged_ref, ordered_ref):
    step = 64

    @pl.loop(0, ordered_ref.shape[0] // step)
    def _(index):
        base = pl.multiple_of(index * step, step)
        rows = [averaged_ref[pl.ds(order_ref[0, base + row], 1), :] for row in range(step)]
        ordered_ref[pl.ds(base, step), :] = jnp.concatenate(rows, axis=0).astype(jnp.bfloat16)


def take_rows(averaged, order):
    return pl.pallas_call(
        order_kernel,
        out_shape=jax.ShapeDtypeStruct(averaged.shape, jnp.bfloat16),
        in_specs=[smem, vmem],
        out_specs=vmem,
        compiler_params=limit(8),
        name="take_rows",
    )(order, averaged)


def arrange_kernel(inverse_ref, spot_ref, arrived_ref, features_ref, half_ref):
    tables, _, width = arrived_ref.shape
    for column in range(tables):
        features_ref[:, column * width : (column + 1) * width] = arrived_ref[inverse_ref[column]]
    start = (1 - spot_ref[0]) * (tables // 2)
    for column in range(tables // 2):
        half_ref[:, column * width : (column + 1) * width] = arrived_ref[inverse_ref[start + column]]


def arrange(arrived, inverse, spot):
    tables, rows, width = arrived.shape
    return pl.pallas_call(
        arrange_kernel,
        out_shape=tuple(
            jax.ShapeDtypeStruct((rows, columns), arrived.dtype)
            for columns in (tables * width, tables * width // 2)
        ),
        in_specs=[smem, smem, vmem],
        out_specs=(vmem, vmem),
        compiler_params=limit(6),
        name="arrange",
    )(inverse, spot, arrived)


def half_kernel(spot_ref, features_ref, half_ref):
    span = half_ref.shape[1]
    start = (1 - spot_ref[0]) * span
    for column in range(0, span, 128):
        columns = pl.ds(pl.multiple_of(start + column, 128), 128)
        half_ref[:, column : column + 128] = features_ref[:, columns]


def near_half(spot, features):
    return pl.pallas_call(
        half_kernel,
        out_shape=jax.ShapeDtypeStruct((features.shape[0], features.shape[1] // 2), features.dtype),
        in_specs=[smem, vmem],
        out_specs=vmem,
        compiler_params=limit(6),
        cost_estimate=pl.CostEstimate(flops=0, bytes_accessed=0, transcendentals=0),
        name="near_half",
    )(spot, features)


def teacher_kernel(features_ref, *refs):
    joined, weights, before, out_ref = refs[:2], refs[2:4], refs[4:-1], refs[-1]
    total = before[0][...] if before else None
    for joined_ref, weights_ref in zip(joined, weights):
        hidden = weights_ref.shape[1]
        held = jnp.maximum(dot(features_ref[...], weights_ref[...]), 0.0).astype(jnp.bfloat16)
        term = dot(held, joined_ref[:hidden, :]) + dot(held, joined_ref[hidden:, :])
        total = term if total is None else total + term
    out_ref[...] = total.astype(out_ref.dtype)


def teacher(features, weights, joined, *before, kept=jnp.float32):
    return pl.pallas_call(
        teacher_kernel,
        out_shape=jax.ShapeDtypeStruct((features.shape[0], joined[0].shape[1]), kept),
        in_specs=[vmem] * (5 + len(before)),
        out_specs=vmem,
        compiler_params=limit(10),
        cost_estimate=pl.CostEstimate(flops=0, bytes_accessed=0, transcendentals=0),
        name="teacher",
    )(features, *joined, *weights, *before)


def student_kernel(
    scale, out_ref, here_ref, there_ref, pre_ref, hidden_ref, weights_ref, loss_ref, grad_ref, second_ref
):
    width = out_ref.shape[1]
    difference = out_ref[...] - (here_ref[...] + there_ref[...].astype(jnp.float32))
    out_grad = (scale * difference).astype(jnp.bfloat16)
    back = lax.dot_general(
        out_grad, weights_ref[...], (((1,), (1,)), ((), ())), preferred_element_type=jnp.float32
    )
    grad_ref[...] = jnp.where(pre_ref[...] > 0, back, 0.0).astype(jnp.bfloat16)
    second_ref[...] = lax.dot_general(
        hidden_ref[...], out_grad, (((0,), (0,)), ((), ())), preferred_element_type=jnp.float32
    ).astype(jnp.bfloat16)
    square = difference * difference
    total = square[:, :128]
    for column in range(128, width, 128):
        total = total + square[:, column : column + 128]
    loss_ref[...] = (0.5 / width) * jnp.sum(total.T, axis=0, keepdims=True)


def student(scale, student_out, here, there, student_pre, student_hidden, student_w2):
    samples, width = student_out.shape
    inner = student_pre.shape[1]
    return pl.pallas_call(
        lambda *refs: student_kernel(scale, *refs),
        out_shape=(
            jax.ShapeDtypeStruct((1, samples), jnp.float32),
            jax.ShapeDtypeStruct((samples, inner), jnp.bfloat16),
            jax.ShapeDtypeStruct((inner, width), jnp.bfloat16),
        ),
        in_specs=[vmem] * 6,
        out_specs=(vmem,) * 3,
        compiler_params=limit(8),
        name="student",
    )(student_out, here, there, student_pre, student_hidden, student_w2)


def turn_kernel(spot_ref, *refs):
    pieces, turned_ref = refs[:-1], refs[-1]
    span = 4 * turned_ref.shape[1]
    high = spot_ref[1]
    for column in range(span // 128):
        whole = pl.ds(pl.multiple_of(spot_ref[0] * span + column * 128, 128), 128)
        half = slice(column * 128, (column + 1) * 128)
        rows = jnp.concatenate(
            [ref[:, half] if ref.shape[1] == span else ref[:, whole] for ref in pieces], axis=0
        )
        for block in range(rows.shape[0] // 128):
            samples = slice(block * 128, (block + 1) * 128)
            turned = rows[samples].astype(jnp.float32).T
            for index in range(2):
                base = index * 64
                kept = jnp.where(
                    high == 0, turned[base : base + 32], turned[base + 32 : base + 64]
                ).astype(jnp.bfloat16)
                place = (2 * column + index) * 16
                for core in range(2):
                    turned_ref[core, place : place + 16, samples] = kept[core * 16 : core * 16 + 16]


def turn(spot, span, *pieces):
    samples = sum(piece.shape[0] for piece in pieces)
    return pl.pallas_call(
        turn_kernel,
        out_shape=jax.ShapeDtypeStruct((2, span // 4, samples), jnp.bfloat16),
        in_specs=[smem] + [vmem] * len(pieces),
        out_specs=vmem,
        compiler_params=limit(8),
        name="turn",
    )(spot, *pieces)


def gradient_kernel(spot_ref, early_ref, late_ref, *refs):
    grads, (mine_ref, other_ref) = refs[:4], refs[4:]
    core = spot_ref[2]
    grad = jnp.concatenate([ref[...] for ref in grads], axis=0)
    early = early_ref.shape[2]
    for ref, place in ((other_ref, 1 - core), (mine_ref, core)):
        total = dot(early_ref[place], grad[:early]) + dot(late_ref[place], grad[early:])
        ref[...] = total.astype(ref.dtype)


def gradients(spot, early, late, grads):
    shape = (early.shape[1], grads[0].shape[1])
    return pl.pallas_call(
        gradient_kernel,
        out_shape=(
            jax.ShapeDtypeStruct(shape, jnp.float32),
            jax.ShapeDtypeStruct(shape, jnp.bfloat16),
        ),
        in_specs=[smem] + [vmem] * 6,
        out_specs=(vmem, vmem),
        compiler_params=limit(8),
        name="gradients",
    )(spot, early, late, *grads)


def shards(
    pooled,
    counts,
    sample_order,
    table_order,
    teacher_w1,
    teacher_w2,
    projection,
    student_w1,
    student_w2,
):
    group = lax.axis_index("grp")
    member = lax.axis_index("mp")
    spot = jnp.stack([group, member // 2, member % 2]).astype(jnp.int32)
    tables = table_order.shape[0]
    block, width = pooled.shape[2:]
    samples = block // tables
    inner, outer = student_w2.shape

    near_w1 = swap(teacher_w1, NEAR)
    core_w1 = swap(teacher_w1, CORE)

    table_range = jnp.arange(tables, dtype=jnp.int32)
    inverse = jnp.sum(
        jnp.where(table_order[None, :] == table_range[:, None], table_range[None, :], 0), axis=1
    )
    divisor = jnp.maximum(counts[0, 0], 1).astype(jnp.float32)
    averaged = pooled[0, 0].astype(jnp.float32) / divisor[:, None]
    ordered = take_rows(averaged, sample_order)
    arrived = lax.all_to_all(
        ordered.reshape(tables, samples, width), "dp", split_axis=0, concat_axis=0, tiled=True
    )

    late_w2, _ = tie(teacher_w2, ordered)
    joined = split_two(dot(late_w2, projection))
    near_joined = swap(joined, NEAR)
    core_joined = swap(joined, CORE)
    arrived, near_w1, joined = tie(arrived, near_w1, joined)

    own, half = arrange(arrived, inverse, spot)
    span = half.shape[1]
    near_core_w1 = swap(near_w1, CORE)
    far = swap(own, FAR)
    near = swap(half, NEAR)

    student_pre = dot(own, student_w1)
    student_hidden = jax.nn.relu(student_pre).astype(jnp.bfloat16)
    student_out = dot(student_hidden, student_w2)
    chip = ((teacher_w1, core_w1), (joined, core_joined))
    here = teacher(own, *chip)

    far, near_joined, here, student_out = tie(far, near_joined, here, student_out)
    next_chip = ((near_w1, near_core_w1), (near_joined, swap(near_joined, CORE)))
    partial = teacher(far, *chip)
    partial = teacher(far, *next_chip, partial, kept=jnp.bfloat16)
    there = swap(partial, FAR)
    opposite = swap(near_half(spot, far), NEAR)
    later_own, _ = tie(own, partial)
    here = teacher(later_own, *next_chip, here)
    there, here, near = tie(there, here, near)
    early = turn(spot, span, own, near, far)

    devices = lax.axis_size("grp") * lax.axis_size("dp") * lax.axis_size("mp")
    grad_scale = 8192.0 / (samples * devices * outer)
    sample_loss, grad, second = student(
        grad_scale, student_out, here, there, student_pre, student_hidden, student_w2
    )
    grads = [grad] + [swap(grad, mask) for mask in (NEAR, FAR, OPPOSITE)]
    opposite, early = tie(opposite, early)
    late = turn(spot, span, opposite)

    second = across(second)
    mine, other = gradients(spot, early, late, grads)
    first = (mine + swap(other, CORE).astype(jnp.float32)).astype(jnp.bfloat16)
    first, second = tie(first, second)
    first = across(first)
    second = total_of(second, tables)
    for mask in (NEAR, OPPOSITE, CORE):
        second = second + swap(second, mask)
    second, first = tie(second, first)
    grad_w1 = total_of(first, tables)
    count = second.shape[0] // 2
    second = lax.dynamic_slice_in_dim(second, spot[2] * count, count, axis=0).astype(jnp.bfloat16)
    second = across(jnp.broadcast_to(second[None], (tables, count, outer)))
    third = swap(second, CORE)
    grad_w2 = jnp.where(
        spot[2] == 0,
        jnp.concatenate([second, third], axis=1),
        jnp.concatenate([third, second], axis=1),
    ).astype(jnp.float32).reshape(inner, outer)
    return (grad_w1, grad_w2, sample_loss)


def solution(mesh):
    return jax.shard_map(
        shards,
        mesh=mesh,
        in_specs=(
            P("dp", LINE, None, None),
            P("dp", LINE, None),
            P(LINE, None),
            P(),
            P(None, LINE),
            P(LINE, None),
            P(),
            P(),
            P(),
        ),
        out_specs=(P(("grp", "dp", "mp"), None), P(), P(LINE, "dp")),
        check_vma=False,
    )
```

```python
import jax
import jax.numpy as jnp
from jax import lax
from jax.experimental import pallas as pl
from jax.experimental.pallas import tpu as pltpu
from jax.sharding import PartitionSpec as P

LINE = ("grp", "mp")
CORE, NEAR, FAR, OPPOSITE = 1, 4, 6, 2

smem = pl.BlockSpec(memory_space=pltpu.SMEM)
vmem = pl.BlockSpec(memory_space=pltpu.VMEM)
anywhere = pl.BlockSpec(memory_space=pl.ANY)


def limit(mebibytes):
    return pltpu.CompilerParams(vmem_limit_bytes=mebibytes * 1024 * 1024)


def tie(*values):
    return lax.optimization_barrier(values)


def dot(left, right):
    return jnp.dot(left, right, preferred_element_type=jnp.float32)


def swap(values, mask):
    return lax.ppermute(values, LINE, [(index, index ^ mask) for index in range(8)])


def split_two(values):
    upper = lax.optimization_barrier(values.astype(jnp.bfloat16))
    lower = (values - upper.astype(jnp.float32)).astype(jnp.bfloat16)
    return jnp.concatenate([upper, lower], axis=0)


def across(values):
    return lax.all_to_all(values, "dp", split_axis=0, concat_axis=0, tiled=True)


def total_of(values, parts):
    return jnp.sum(values.reshape(parts, -1, values.shape[1]).astype(jnp.float32), axis=0)


def order_kernel(order_ref, averaged_ref, ordered_ref):
    step = 64

    @pl.loop(0, ordered_ref.shape[0] // step)
    def _(index):
        base = pl.multiple_of(index * step, step)
        rows = [averaged_ref[pl.ds(order_ref[0, base + row], 1), :] for row in range(step)]
        ordered_ref[pl.ds(base, step), :] = jnp.concatenate(rows, axis=0).astype(jnp.bfloat16)


def take_rows(averaged, order):
    return pl.pallas_call(
        order_kernel,
        out_shape=jax.ShapeDtypeStruct(averaged.shape, jnp.bfloat16),
        in_specs=[smem, vmem],
        out_specs=vmem,
        compiler_params=limit(8),
        name="take_rows",
    )(order, averaged)


def arrange_kernel(inverse_ref, spot_ref, arrived_ref, features_ref, half_ref):
    tables, _, width = arrived_ref.shape
    for column in range(tables):
        features_ref[:, column * width : (column + 1) * width] = arrived_ref[inverse_ref[column]]
    start = (1 - spot_ref[0]) * (tables // 2)
    for column in range(tables // 2):
        half_ref[:, column * width : (column + 1) * width] = arrived_ref[inverse_ref[start + column]]


def arrange(arrived, inverse, spot):
    tables, rows, width = arrived.shape
    return pl.pallas_call(
        arrange_kernel,
        out_shape=tuple(
            jax.ShapeDtypeStruct((rows, columns), arrived.dtype)
            for columns in (tables * width, tables * width // 2)
        ),
        in_specs=[smem, smem, vmem],
        out_specs=(vmem, vmem),
        compiler_params=limit(6),
        name="arrange",
    )(inverse, spot, arrived)


def half_kernel(spot_ref, features_ref, half_ref):
    span = half_ref.shape[1]
    start = (1 - spot_ref[0]) * span
    for column in range(0, span, 128):
        columns = pl.ds(pl.multiple_of(start + column, 128), 128)
        half_ref[:, column : column + 128] = features_ref[:, columns]


def near_half(spot, features):
    return pl.pallas_call(
        half_kernel,
        out_shape=jax.ShapeDtypeStruct((features.shape[0], features.shape[1] // 2), features.dtype),
        in_specs=[smem, vmem],
        out_specs=vmem,
        compiler_params=limit(6),
        cost_estimate=pl.CostEstimate(flops=0, bytes_accessed=0, transcendentals=0),
        name="near_half",
    )(spot, features)


def teacher_kernel(features_ref, *refs):
    joined, weights, before, out_ref = refs[:2], refs[2:4], refs[4:-1], refs[-1]
    total = before[0][...] if before else None
    for joined_ref, weights_ref in zip(joined, weights):
        hidden = weights_ref.shape[1]
        held = jnp.maximum(dot(features_ref[...], weights_ref[...]), 0.0).astype(jnp.bfloat16)
        term = dot(held, joined_ref[:hidden, :]) + dot(held, joined_ref[hidden:, :])
        total = term if total is None else total + term
    out_ref[...] = total.astype(out_ref.dtype)


def teacher(features, weights, joined, *before, kept=jnp.float32):
    return pl.pallas_call(
        teacher_kernel,
        out_shape=jax.ShapeDtypeStruct((features.shape[0], joined[0].shape[1]), kept),
        in_specs=[vmem] * (5 + len(before)),
        out_specs=vmem,
        compiler_params=limit(10),
        cost_estimate=pl.CostEstimate(flops=0, bytes_accessed=0, transcendentals=0),
        name="teacher",
    )(features, *joined, *weights, *before)


def student_kernel(
    scale, out_ref, here_ref, there_ref, pre_ref, hidden_ref, weights_ref, loss_ref, grad_ref, second_ref
):
    width = out_ref.shape[1]
    difference = out_ref[...] - (here_ref[...] + there_ref[...].astype(jnp.float32))
    out_grad = (scale * difference).astype(jnp.bfloat16)
    back = lax.dot_general(
        out_grad, weights_ref[...], (((1,), (1,)), ((), ())), preferred_element_type=jnp.float32
    )
    grad_ref[...] = jnp.where(pre_ref[...] > 0, back, 0.0).astype(jnp.bfloat16)
    second_ref[...] = lax.dot_general(
        hidden_ref[...], out_grad, (((0,), (0,)), ((), ())), preferred_element_type=jnp.float32
    ).astype(jnp.bfloat16)
    square = difference * difference
    total = square[:, :128]
    for column in range(128, width, 128):
        total = total + square[:, column : column + 128]
    loss_ref[...] = (0.5 / width) * jnp.sum(total.T, axis=0, keepdims=True)


def student(scale, student_out, here, there, student_pre, student_hidden, student_w2):
    samples, width = student_out.shape
    inner = student_pre.shape[1]
    return pl.pallas_call(
        lambda *refs: student_kernel(scale, *refs),
        out_shape=(
            jax.ShapeDtypeStruct((1, samples), jnp.float32),
            jax.ShapeDtypeStruct((samples, inner), jnp.bfloat16),
            jax.ShapeDtypeStruct((inner, width), jnp.bfloat16),
        ),
        in_specs=[vmem] * 6,
        out_specs=(vmem,) * 3,
        compiler_params=limit(8),
        name="student",
    )(student_out, here, there, student_pre, student_hidden, student_w2)


def turn_kernel(spot_ref, *refs):
    pieces, turned_ref = refs[:-1], refs[-1]
    span = 4 * turned_ref.shape[1]
    high = spot_ref[1]
    for column in range(span // 128):
        whole = pl.ds(pl.multiple_of(spot_ref[0] * span + column * 128, 128), 128)
        half = slice(column * 128, (column + 1) * 128)
        rows = jnp.concatenate(
            [ref[:, half] if ref.shape[1] == span else ref[:, whole] for ref in pieces], axis=0
        )
        for block in range(rows.shape[0] // 128):
            samples = slice(block * 128, (block + 1) * 128)
            turned = rows[samples].astype(jnp.float32).T
            for index in range(2):
                base = index * 64
                kept = jnp.where(
                    high == 0, turned[base : base + 32], turned[base + 32 : base + 64]
                ).astype(jnp.bfloat16)
                place = (2 * column + index) * 16
                for core in range(2):
                    turned_ref[core, place : place + 16, samples] = kept[core * 16 : core * 16 + 16]


def turn(spot, span, *pieces):
    samples = sum(piece.shape[0] for piece in pieces)
    return pl.pallas_call(
        turn_kernel,
        out_shape=jax.ShapeDtypeStruct((2, span // 4, samples), jnp.bfloat16),
        in_specs=[smem] + [vmem] * len(pieces),
        out_specs=vmem,
        compiler_params=limit(8),
        name="turn",
    )(spot, *pieces)


def gradient_kernel(spot_ref, early_ref, late_ref, *refs):
    grads, (mine_ref, other_ref) = refs[:4], refs[4:]
    core = spot_ref[2]
    grad = jnp.concatenate([ref[...] for ref in grads], axis=0)
    early = early_ref.shape[2]
    for ref, place in ((other_ref, 1 - core), (mine_ref, core)):
        total = dot(early_ref[place], grad[:early]) + dot(late_ref[place], grad[early:])
        ref[...] = total.astype(ref.dtype)


def gradients(spot, early, late, grads):
    shape = (early.shape[1], grads[0].shape[1])
    return pl.pallas_call(
        gradient_kernel,
        out_shape=(
            jax.ShapeDtypeStruct(shape, jnp.float32),
            jax.ShapeDtypeStruct(shape, jnp.bfloat16),
        ),
        in_specs=[smem] + [vmem] * 6,
        out_specs=(vmem, vmem),
        compiler_params=limit(8),
        name="gradients",
    )(spot, early, late, *grads)


def shards(
    pooled,
    counts,
    sample_order,
    table_order,
    teacher_w1,
    teacher_w2,
    projection,
    student_w1,
    student_w2,
):
    group = lax.axis_index("grp")
    member = lax.axis_index("mp")
    spot = jnp.stack([group, member // 2, member % 2]).astype(jnp.int32)
    tables = table_order.shape[0]
    block, width = pooled.shape[2:]
    samples = block // tables
    inner, outer = student_w2.shape

    near_w1 = swap(teacher_w1, NEAR)
    core_w1 = swap(teacher_w1, CORE)

    table_range = jnp.arange(tables, dtype=jnp.int32)
    inverse = jnp.sum(
        jnp.where(table_order[None, :] == table_range[:, None], table_range[None, :], 0), axis=1
    )
    divisor = jnp.maximum(counts[0, 0], 1).astype(jnp.float32)
    averaged = pooled[0, 0].astype(jnp.float32) / divisor[:, None]
    ordered = take_rows(averaged, sample_order)
    arrived = lax.all_to_all(
        ordered.reshape(tables, samples, width), "dp", split_axis=0, concat_axis=0, tiled=True
    )

    late_w2, _ = tie(teacher_w2, ordered)
    joined = split_two(dot(late_w2, projection))
    near_joined = swap(joined, NEAR)
    core_joined = swap(joined, CORE)
    arrived, near_w1, joined = tie(arrived, near_w1, joined)

    own, half = arrange(arrived, inverse, spot)
    span = half.shape[1]
    near_core_w1 = swap(near_w1, CORE)
    far = swap(own, FAR)
    near = swap(half, NEAR)

    student_pre = dot(own, student_w1)
    student_hidden = jax.nn.relu(student_pre).astype(jnp.bfloat16)
    student_out = dot(student_hidden, student_w2)
    chip = ((teacher_w1, core_w1), (joined, core_joined))
    here = teacher(own, *chip)

    far, near_joined, here, student_out = tie(far, near_joined, here, student_out)
    next_chip = ((near_w1, near_core_w1), (near_joined, swap(near_joined, CORE)))
    partial = teacher(far, *chip)
    partial = teacher(far, *next_chip, partial, kept=jnp.bfloat16)
    there = swap(partial, FAR)
    later_far, partial = tie(far, partial)
    opposite = swap(near_half(spot, later_far), NEAR)
    later_own, _ = tie(own, partial)
    here = teacher(later_own, *next_chip, here)
    there, here, near = tie(there, here, near)
    early = turn(spot, span, own, near, far)

    devices = lax.axis_size("grp") * lax.axis_size("dp") * lax.axis_size("mp")
    grad_scale = 8192.0 / (samples * devices * outer)
    sample_loss, grad, second = student(
        grad_scale, student_out, here, there, student_pre, student_hidden, student_w2
    )
    grads = [grad] + [swap(grad, mask) for mask in (NEAR, FAR, OPPOSITE)]
    opposite, early = tie(opposite, early)
    late = turn(spot, span, opposite)

    second = across(second)
    mine, other = gradients(spot, early, late, grads)
    first = (mine + swap(other, CORE).astype(jnp.float32)).astype(jnp.bfloat16)
    first, second = tie(first, second)
    first = across(first)
    second = total_of(second, tables)
    for mask in (NEAR, OPPOSITE, CORE):
        second = second + swap(second, mask)
    second, first = tie(second, first)
    grad_w1 = total_of(first, tables)
    count = second.shape[0] // 2
    second = lax.dynamic_slice_in_dim(second, spot[2] * count, count, axis=0).astype(jnp.bfloat16)
    second = across(jnp.broadcast_to(second[None], (tables, count, outer)))
    third = swap(second, CORE)
    grad_w2 = jnp.where(
        spot[2] == 0,
        jnp.concatenate([second, third], axis=1),
        jnp.concatenate([third, second], axis=1),
    ).astype(jnp.float32).reshape(inner, outer)
    return (grad_w1, grad_w2, sample_loss)


def solution(mesh):
    return jax.shard_map(
        shards,
        mesh=mesh,
        in_specs=(
            P("dp", LINE, None, None),
            P("dp", LINE, None),
            P(LINE, None),
            P(),
            P(None, LINE),
            P(LINE, None),
            P(),
            P(),
            P(),
        ),
        out_specs=(P(("grp", "dp", "mp"), None), P(), P(LINE, "dp")),
        check_vma=False,
    )
```
